32 devices in a mesh: node: 8 (over z, y), local: 4 (over x, core).
Axes of the slice: x: 2, y: 2, z: 4, core: 2. Of those that a mesh axis runs over, the one named last changes fastest.
Arguments:
- tokens: bfloat16 [256, 4096], P('node', 'local'), may hold values from -6 to 6
- node_ids: int32 [256, 4], P('node'), may hold values from 0 to 7, all different within a row; in each aligned block of 32 rows (0 to 31, 32 to 63, ...) at most 32 rows name the same one
- mix_weights: float32 [256, 4], P('node'), may hold values from 0.05 to 1
- w_gate: bfloat16 [8, 4096, 1024], P('node', 'local'), may hold values from -0.09375 to 0.09375
- w_up: bfloat16 [8, 4096, 1024], P('node', 'local'), may hold values from -0.09375 to 0.09375
- w_down: bfloat16 [8, 1024, 4096], P('node', None, 'local'), may hold values from -0.1875 to 0.1875
Outputs:
- mixed: bfloat16 [256, 4096], P('node', 'local')
The draws below stay inside these ranges and needn't reach their ends.
Inputs may be any that keep to these rules, and one draw needn't show every extreme that they name: `node_ids`: each row names 4 different experts. Among the 32 tokens of one node (aligned blocks of rows), at most 32 name the same expert, and in every draw some expert is named by exactly 32 tokens of some node.
All inputs are finite; a program needn't handle non-finite values.
Results may differ from the reference program's by a relative error of at most 0.023.
Values may be sent and summed in bfloat16 or wider, within the bound.
A program may use at most 64 MiB of HBM per device.

```python
import math
import jax
import jax.numpy as jnp
import numpy as np
from jax import lax

D = 4096
HID = 1024
TOP = 4
TOK_NODE = 32
EXPERTS = 8
CAP = 32
TOKENS = 256
N_NODE = 8
N_LOCAL = 4


def level_of(key, shape, shards, smallest, top_value):
    level = 1.0
    for dim, blocks in shards:
        heights = jax.random.uniform(jax.random.fold_in(jax.random.fold_in(key, 6), dim), (blocks,), jnp.float32, smallest / len(shards), top_value / len(shards))
        level = level * jnp.repeat(jnp.exp(heights), shape[dim] // blocks).reshape((-1,) + (1,) * (len(shape) - 1 - dim))
    return level


def shared_out(own_key, own, number, rows, amount, top, limit, skew):
    order = jax.random.permutation(own_key, amount)
    packed, ordinary = portions_of(amount, rows * top, limit, skew, True), portions_of(amount, rows * top, limit, skew, False)
    places = jnp.arange(amount)

    def named(sizes, rotation):
        used = int((sizes > 0).sum())
        fixed = max(1, used // 4)
        moved = fixed + (places - fixed + rotation * (used - fixed)) % max(1, amount - fixed)
        return jnp.zeros((amount,), jnp.int32).at[order[jnp.where(places < fixed, places, moved)]].set(jnp.asarray(sizes, jnp.int32))

    sizes = jnp.where(number % 4 == 0, named(packed, number // 4), named(ordinary, number - number // 4 - 1))
    mixed = jax.random.permutation(jax.random.fold_in(own, 3), amount)
    donor, receiver = mixed[0:amount // 2 * 2:2], mixed[1:amount // 2 * 2:2]
    slack = jnp.minimum(sizes[donor] - 1, limit - sizes[receiver]) // 2
    slack = jnp.where((donor == order[0]) | (receiver == order[0]) | (sizes[receiver] == 0), 0, jnp.maximum(slack, 0))
    moved = jax.random.randint(jax.random.fold_in(own, 4), (amount // 2,), 0, 1 << 20) % (slack + 1)
    sizes = sizes.at[donor].add(-moved).at[receiver].add(moved)
    items = jnp.searchsorted(jnp.cumsum(sizes), jnp.arange(rows * top), side="right").astype(jnp.int32)
    listing = items.reshape(top, rows).T
    listing = listing[jax.random.permutation(jax.random.fold_in(own, 1), rows)]
    rotation = jax.random.randint(jax.random.fold_in(own, 2), (rows, 1), 0, top)
    return jnp.take_along_axis(listing, (jnp.arange(top)[None, :] + rotation) % top, axis=1)


def portions_of(number_of, total, bound, slope, full):
    loads = [(1 << 20) // math.isqrt(standing ** slope) + 1 for standing in range(1, number_of + 1)]
    largest = bound if full else min(bound, max(-(-total // number_of), total * loads[0] // sum(loads)))
    least = 1 if total - largest >= number_of - 1 else 0
    given, rest = [largest] + [least] * (number_of - 1), total - largest - least * (number_of - 1)
    while rest > 0:
        free = [i for i in range(1, number_of) if given[i] < largest] or [i for i in range(1, number_of) if given[i] < bound]
        mass, remaining = sum([loads[i] for i in free]), rest
        for i in free:
            addition = min(bound - given[i], max(1, remaining * loads[i] // mass), rest)
            given[i] = given[i] + addition
            rest = rest - addition
    return np.array(given)


def normal_values(rng, dims, deviation, bound, cuts=(), held_as=jnp.bfloat16):
    drawn = jax.random.normal(rng, dims, jnp.float32) * deviation
    if len(cuts) > 0:
        drawn = level_of(rng, dims, cuts, -0.22, 0.18) * drawn
    return jnp.clip(drawn, min=-bound, max=bound).astype(held_as)


def setup_inputs(seed: int = 0) -> dict:
    arg_keys = jax.random.split(jax.random.key(seed), 7)
    tokens = normal_values(arg_keys[0], (TOKENS, D), 1.0, 6.0, ((0, 8), (1, 4)))
    node_ids_keys = jax.random.split(jax.random.fold_in(arg_keys[1], 1), TOKENS // TOK_NODE)
    node_ids_turns = jax.random.permutation(jax.random.fold_in(arg_keys[1], 3), TOKENS // TOK_NODE)
    node_ids = jax.vmap(lambda own, number: shared_out(jax.random.fold_in(arg_keys[1], 2), own, number, TOK_NODE, EXPERTS, TOP, CAP, 2))(node_ids_keys, node_ids_turns).reshape((TOKENS, TOP))
    mix_weights = jnp.clip(jnp.exp(math.log(1.0) - 2.9957323 * jax.random.uniform(arg_keys[2], (TOKENS, TOP), jnp.float32) ** level_of(arg_keys[2], (TOKENS, TOP), ((0, 8),), -0.2, 0.2)), 0.05, 1.0)
    w_gate = normal_values(arg_keys[3], (EXPERTS, D, HID), D ** -0.5, 0.09375, ((0, 8), (1, 4)))
    w_up = normal_values(arg_keys[4], (EXPERTS, D, HID), D ** -0.5, 0.09375, ((0, 8), (1, 4)))
    w_down = normal_values(arg_keys[5], (EXPERTS, HID, D), HID ** -0.5, 0.1875, ((0, 8), (2, 4)))
    return {"tokens": tokens, "node_ids": node_ids, "mix_weights": mix_weights, "w_gate": w_gate, "w_up": w_up, "w_down": w_down}


def reference(tokens, node_ids, mix_weights, w_gate, w_up, w_down):
    count = TOKENS * TOP
    flat_ids = node_ids.reshape(-1)
    owners = jnp.arange(count, dtype=jnp.int32) // TOP
    flat_mix = mix_weights.reshape(-1)
    split = D // N_LOCAL
    room = N_NODE * CAP

    def slice_sum(pieces, weight):
        parts = jnp.einsum('snd,ndh->nsh', pieces, weight.reshape(N_LOCAL, split, HID).astype(jnp.float32), precision=lax.Precision.HIGHEST)
        rounded = lax.optimization_barrier(parts.astype(jnp.bfloat16))
        return jnp.sum(rounded.astype(jnp.float32), axis=0)

    def one_expert(total, expert):
        chosen = flat_ids == expert
        index = jnp.nonzero(chosen, size=room, fill_value=0)[0].astype(jnp.int32)
        valid = (jnp.arange(room, dtype=jnp.int32) < jnp.sum(chosen.astype(jnp.int32))).astype(jnp.float32)
        owner_rows = owners[index]
        rows_in = tokens[owner_rows]
        pieces = rows_in.reshape(room, N_LOCAL, split).astype(jnp.float32)
        gate = slice_sum(pieces, w_gate[expert])
        up = slice_sum(pieces, w_up[expert])
        active = (jax.nn.silu(gate) * up).astype(jnp.bfloat16)
        result = jnp.dot(active, w_down[expert], preferred_element_type=jnp.float32).astype(jnp.bfloat16)
        result = lax.optimization_barrier(result).astype(jnp.float32)
        scaled = result * (flat_mix[index] * valid)[:, None]
        return total.at[owner_rows].add(scaled), None

    start = jnp.zeros((TOKENS, D), jnp.float32)
    total, unused = lax.scan(one_expert, start, jnp.arange(EXPERTS, dtype=jnp.int32))
    return total.astype(jnp.bfloat16)
```

```python
import functools

import jax
import jax.numpy as jnp
from jax import lax
from jax.experimental import pallas as pl
from jax.experimental.pallas import tpu as pltpu
from jax.sharding import PartitionSpec as P

PAIR = 2
LANES = 128
F32 = jnp.float32
BF16 = jnp.bfloat16


def partner(index, step, count):
    if count & (count - 1):
        return lax.rem(index + step, count)
    result, bit = 0, 1
    while bit < count:
        digit = lax.rem(index // bit, 2)
        result = result + (1 - digit if step & bit else digit) * bit
        bit *= 2
    return result


def fused_kernel(
    tok, ids, mix, wg, wu, wd, out,
    xbuf, vg, vu, vd, psend, precv, pown, xsend, xrecv, act, ysend, ykeep, yrecv,
    zsend, zrecv, zown,
    load_sem, a_zsend, a_ysend, a_recv, p_send, p_recv, x_send, x_recv,
    t_send, t_recv, y_send, y_recv, z_send, z_recv,
):
    node_count, row_count, wide = xbuf.shape
    feat = wide - LANES
    groups = node_count // PAIR
    rows = PAIR * row_count
    hid = vg.shape[1]
    half, quarter = hid // PAIR, hid // (PAIR * PAIR)
    feat_out = vd.shape[1]
    node, local = lax.axis_index("node"), lax.axis_index("local")
    z, y = node // PAIR, lax.rem(node, PAIR)
    x, c = local // PAIR, lax.rem(local, PAIR)
    mine = c * PAIR + x

    def at(zz, yy, xx, cc):
        return {"node": zz * PAIR + yy, "local": xx * PAIR + cc}

    y_peer, c_peer, x_peer = at(z, 1 - y, x, c), at(z, y, x, 1 - c), at(z, y, 1 - x, c)
    d_peer = at(z, y, 1 - x, 1 - c)
    z_peers = [at(partner(z, s, groups), y, x, c) for s in range(1, groups)]
    planes = [partner(z, s, groups) for s in range(groups)]

    def remote(src, dst, send, recv, device):
        return pltpu.make_async_remote_copy(
            src_ref=src, dst_ref=dst, send_sem=send, recv_sem=recv,
            device_id=device, device_id_type=pl.DeviceIdType.MESH,
        )

    loads = [
        pltpu.make_async_copy(tok, xbuf.at[node, :, pl.ds(0, feat)], load_sem.at[0]),
        pltpu.make_async_copy(wg.at[0], vg, load_sem.at[1]),
        pltpu.make_async_copy(wu.at[0], vu, load_sem.at[2]),
        pltpu.make_async_copy(wd.at[0], vd, load_sem.at[3]),
    ]
    for load in loads:
        load.start()
    barrier = pltpu.get_barrier_semaphore()
    peers = [y_peer, c_peer, x_peer, d_peer] + z_peers
    for peer in peers:
        pl.semaphore_signal(barrier, inc=1, device_id=peer, device_id_type=pl.DeviceIdType.MESH)

    lane = lax.broadcasted_iota(jnp.int32, (row_count, LANES), 1)
    weight = jnp.zeros((row_count, LANES), F32)
    for k in range(ids.shape[1]):
        expert = ids[:, k : k + 1]
        weight += jnp.where(
            (lane == expert) | (lane == expert + node_count), mix[:, k : k + 1], 0.0
        )
    head = weight.astype(BF16).astype(F32)
    xbuf[node, :, feat:] = jnp.where(lane < node_count, head, weight - head).astype(BF16)
    loads[0].wait()
    pl.semaphore_wait(barrier, len(peers))

    pending = []

    def launch(copy):
        copy.start()
        pending.append(copy)

    launch(remote(xbuf.at[node], xbuf.at[node], a_ysend.at[0], a_recv.at[node], y_peer))
    for s in range(1, groups):
        launch(
            remote(xbuf.at[node], xbuf.at[node], a_zsend.at[s], a_recv.at[node], z_peers[s - 1])
        )

    def forward(s):
        if not 0 < s < groups:
            return
        origin = planes[s] * PAIR + y
        copy = remote(xbuf.at[origin], xbuf.at[origin], a_ysend.at[s], a_recv.at[origin], y_peer)
        copy.wait_recv()
        launch(copy)

    def project(s):
        origin = planes[s] * PAIR + 1 - y
        remote(
            xbuf.at[origin], xbuf.at[origin], a_ysend.at[s], a_recv.at[origin], y_peer
        ).wait_recv()
        if s == 0:
            loads[1].wait()
            loads[2].wait()
        inputs = xbuf[pl.ds(planes[s] * PAIR, PAIR), :, :feat].reshape(rows, feat)
        for target, first in ((psend, (1 - c) * half), (pown, c * half)):
            for part in range(PAIR):
                cols = pl.ds(pl.multiple_of(first + part * quarter, quarter), quarter)
                for which, matrix in enumerate((vg, vu)):
                    product = jnp.dot(inputs, matrix[:, cols], preferred_element_type=F32)
                    start = (part * 2 + which) * quarter
                    target[s, :, start : start + quarter] = product.astype(target.dtype)
            if target is psend:
                launch(remote(psend.at[s], precv.at[s], p_send.at[s], p_recv.at[s], c_peer))

    def cross(s):
        remote(psend.at[s], precv.at[s], p_send.at[s], p_recv.at[s], c_peer).wait_recv()
        cols = pl.ds(pl.multiple_of((1 - x) * 2 * quarter, 2 * quarter), 2 * quarter)
        xsend[s] = (pown[s, :, cols] + precv[s, :, cols].astype(F32)).astype(BF16)
        launch(remote(xsend.at[s], xrecv.at[s], x_send.at[s], x_recv.at[s], x_peer))

    def activate(s):
        remote(xsend.at[s], xrecv.at[s], x_send.at[s], x_recv.at[s], x_peer).wait_recv()
        cols = pl.ds(pl.multiple_of(x * 2 * quarter, 2 * quarter), 2 * quarter)
        total = pown[s, :, cols] + precv[s, :, cols].astype(F32) + xrecv[s].astype(F32)
        gate, up = total[:, :quarter], total[:, quarter:]
        act[s, mine] = (gate / (1.0 + jnp.exp(-gate)) * up).astype(BF16)
        for k, peer in enumerate((d_peer, x_peer, c_peer)):
            launch(
                remote(act.at[s, mine], act.at[s, mine], t_send.at[s, k], t_recv.at[s, mine], peer)
            )

    def down(s):
        for k, (cc, xx) in enumerate(((1 - c, 1 - x), (c, 1 - x), (1 - c, x))):
            slot = cc * PAIR + xx
            remote(
                act.at[s, slot], act.at[s, slot], t_send.at[s, k], t_recv.at[s, slot], d_peer
            ).wait_recv()
        if s == 0:
            loads[3].wait()
        hidden = jnp.concatenate([act[s, q] for q in range(PAIR * PAIR)], axis=1)
        scales = xbuf[pl.ds(planes[s] * PAIR, PAIR), :, feat:].reshape(rows, LANES).astype(F32)
        lanes = lax.broadcasted_iota(jnp.int32, (rows, LANES), 1)
        mine_only = (lanes == node) | (lanes == node + node_count)
        scale = jnp.sum(jnp.where(mine_only, scales, 0.0), axis=1, keepdims=True)
        step = min(feat_out, 2 * LANES)
        for start in range(0, feat_out, step):
            result = jnp.dot(hidden, vd[:, start : start + step], preferred_element_type=F32)
            scaled = (result.astype(BF16).astype(F32) * scale).reshape(PAIR, row_count, step)
            ykeep[s, :, :, start : start + step] = scaled
            ysend[s, :, :, start : start + step] = scaled.astype(BF16)
        launch(remote(ysend.at[s, 1 - y], yrecv.at[s], y_send.at[s], y_recv.at[s], y_peer))

    def give_back(s):
        remote(ysend.at[s, 1 - y], yrecv.at[s], y_send.at[s], y_recv.at[s], y_peer).wait_recv()
        total = ykeep[s, y] + yrecv[s].astype(F32)
        if s == 0:
            zown[...] = total
        else:
            zsend[s] = total.astype(BF16)
            launch(remote(zsend.at[s], zrecv.at[z], z_send.at[s], z_recv.at[z], z_peers[s - 1]))

    forward(1)
    stages = (project, cross, activate, down, give_back)
    for slot in range(groups + len(stages) - 1):
        for delay, stage in enumerate(stages):
            if 0 <= slot - delay < groups:
                stage(slot - delay)
            if delay == 0:
                forward(slot + 2)

    total = zown[...]
    for s in range(1, groups):
        origin = planes[s]
        remote(
            zsend.at[s], zrecv.at[origin], z_send.at[s], z_recv.at[origin], z_peers[s - 1]
        ).wait_recv()
        total = total + zrecv[origin].astype(F32)
    out[...] = total.astype(BF16)
    for copy in pending:
        copy.wait_send()


def fused_body(tokens, node_ids, mix_weights, w_gate, w_up, w_down):
    row_count, feat = tokens.shape
    node_count = lax.axis_size("node")
    hid, feat_out = w_down.shape[1], w_down.shape[2]
    groups, rows = node_count // PAIR, PAIR * row_count
    half = hid // PAIR
    quarters = PAIR * PAIR
    anywhere = pl.BlockSpec(memory_space=pl.ANY)
    vmem = pl.BlockSpec(memory_space=pltpu.VMEM)
    dma = pltpu.SemaphoreType.DMA
    return pl.pallas_call(
        fused_kernel,
        out_shape=jax.ShapeDtypeStruct((row_count, feat_out), BF16),
        in_specs=[anywhere, vmem, vmem, anywhere, anywhere, anywhere],
        out_specs=vmem,
        scratch_shapes=[
            pltpu.VMEM((node_count, row_count, feat + LANES), BF16),
            pltpu.VMEM((feat, hid), BF16),
            pltpu.VMEM((feat, hid), BF16),
            pltpu.VMEM((hid, feat_out), BF16),
            pltpu.VMEM((groups, rows, 2 * half), BF16),
            pltpu.VMEM((groups, rows, 2 * half), BF16),
            pltpu.VMEM((groups, rows, 2 * half), F32),
            pltpu.VMEM((groups, rows, half), BF16),
            pltpu.VMEM((groups, rows, half), BF16),
            pltpu.VMEM((groups, quarters, rows, hid // quarters), BF16),
            pltpu.VMEM((groups, PAIR, row_count, feat_out), BF16),
            pltpu.VMEM((groups, PAIR, row_count, feat_out), F32),
            pltpu.VMEM((groups, row_count, feat_out), BF16),
            pltpu.VMEM((groups, row_count, feat_out), BF16),
            pltpu.VMEM((groups, row_count, feat_out), BF16),
            pltpu.VMEM((row_count, feat_out), F32),
            dma((4,)),
            dma((groups,)),
            dma((groups,)),
            dma((node_count,)),
            dma((groups,)),
            dma((groups,)),
            dma((groups,)),
            dma((groups,)),
            dma((groups, quarters - 1)),
            dma((groups, quarters)),
            dma((groups,)),
            dma((groups,)),
            dma((groups,)),
            dma((groups,)),
        ],
        compiler_params=pltpu.CompilerParams(
            collective_id=0, has_side_effects=True, vmem_limit_bytes=40 * 1024 * 1024
        ),
        cost_estimate=pl.CostEstimate(
            flops=2 * node_count * row_count * hid * (2 * feat + feat_out),
            bytes_accessed=2 * hid * (2 * feat + feat_out),
            transcendentals=node_count * row_count * hid // quarters,
        ),
    )(tokens, node_ids, mix_weights, w_gate, w_up, w_down)


def slot_body(slot_cap, tokens, node_ids, mix_weights, w_gate, w_up, w_down):
    row_count, feat_width = tokens.shape
    pick_count = node_ids.shape[1]
    node_count = lax.axis_size("node")
    slot_total = node_count * slot_cap
    flat_ids = node_ids.reshape(-1)
    hit_table = (flat_ids[:, None] == jnp.arange(node_count, dtype=jnp.int32)[None, :]).astype(
        jnp.int32
    )
    earlier = jnp.cumsum(hit_table, axis=0) - hit_table
    slot_rank = jnp.sum(earlier * hit_table, axis=1)
    position = flat_ids * slot_cap + slot_rank
    slot_table = jnp.arange(slot_total, dtype=jnp.int32)[:, None] == position[None, :]
    dispatch = jnp.any(slot_table.reshape(slot_total, row_count, pick_count), axis=2).astype(
        jnp.bfloat16
    )
    outbound = jnp.dot(dispatch, tokens, preferred_element_type=jnp.float32).astype(jnp.bfloat16)
    outbound = outbound.reshape(node_count, slot_cap, feat_width)
    inbound = lax.all_to_all(outbound, "node", split_axis=0, concat_axis=0, tiled=True)
    inbound = inbound.reshape(slot_total, feat_width)
    gate_part = jnp.dot(inbound, w_gate[0], preferred_element_type=jnp.float32)
    up_part = jnp.dot(inbound, w_up[0], preferred_element_type=jnp.float32)
    gate_whole, up_whole = (
        lax.psum(gate_part.astype(jnp.bfloat16), "local").astype(jnp.float32),
        lax.psum(up_part.astype(jnp.bfloat16), "local").astype(jnp.float32),
    )
    active = (jax.nn.silu(gate_whole) * up_whole).astype(jnp.bfloat16)
    result = jnp.dot(active, w_down[0], preferred_element_type=jnp.float32)
    expert_out = result.astype(jnp.bfloat16).reshape(node_count, slot_cap, feat_width)
    returned = lax.all_to_all(expert_out, "node", split_axis=0, concat_axis=0, tiled=True)
    returned = returned.reshape(slot_total, feat_width)
    weighting = slot_table.astype(jnp.float32) * mix_weights.reshape(-1)[None, :]
    combine = jnp.sum(weighting.reshape(slot_total, row_count, pick_count), axis=2)
    mixed = lax.dot_general(
        combine,
        returned.astype(jnp.float32),
        (((0,), (0,)), ((), ())),
        precision=lax.Precision.HIGHEST,
    )
    return mixed.astype(jnp.bfloat16)


def body(tokens, node_ids, mix_weights, w_gate, w_up, w_down):
    row_count, pick_count = node_ids.shape
    node_count, local_count = lax.axis_size("node"), lax.axis_size("local")
    slot_cap = max(2, 2 * row_count * pick_count // node_count)
    args = (tokens, node_ids, mix_weights, w_gate, w_up, w_down)
    whole_rows = slot_cap >= row_count and node_count % PAIR == 0 and 2 * node_count <= LANES
    if whole_rows and local_count == PAIR * PAIR:
        return fused_body(*args)
    return slot_body(slot_cap, *args)


def solution(mesh):
    return jax.shard_map(
        body,
        mesh=mesh,
        in_specs=(
            P("node", "local"),
            P("node", None),
            P("node", None),
            P("node", "local", None),
            P("node", "local", None),
            P("node", None, "local"),
        ),
        out_specs=P("node", "local"),
        check_vma=False,
    )
```

```python
import functools

import jax
import jax.numpy as jnp
from jax import lax
from jax.experimental import pallas as pl
from jax.experimental.pallas import tpu as pltpu
from jax.sharding import PartitionSpec as P

PAIR = 2
LANES = 128
VMEM_BYTES = 60 * 1024 * 1024
F32 = jnp.float32
BF16 = jnp.bfloat16


def partner(index, step, count):
    if count & (count - 1):
        return lax.rem(index + step, count)
    result, bit = 0, 1
    while bit < count:
        digit = lax.rem(index // bit, 2)
        result = result + (1 - digit if step & bit else digit) * bit
        bit *= 2
    return result


def chunks_of(groups):
    count = min(groups, 2)
    return [list(range(first, groups, count))[::-1] for first in range(count)]


def fused_kernel(
    tok, ids, mix, wg, wu, wd, out,
    xbuf, vg, vu, vd, psend, precv, pown, xsend, xrecv, act, ysend, ykeep, yrecv,
    zsend, zrecv, zown,
    load_sem, a_zsend, a_ysend, a_recv, p_send, p_recv, x_send, x_recv,
    t_send, t_recv, y_send, y_recv, z_send, z_recv,
):
    node_count, row_count, wide = xbuf.shape
    feat = wide - LANES
    groups = node_count // PAIR
    chunks = chunks_of(groups)
    hid = vg.shape[1]
    half, quarter = hid // PAIR, hid // (PAIR * PAIR)
    feat_out = vd.shape[1]
    node, local = lax.axis_index("node"), lax.axis_index("local")
    z, y = node // PAIR, lax.rem(node, PAIR)
    x, c = local // PAIR, lax.rem(local, PAIR)
    mine = c * PAIR + x

    def at(zz, yy, xx, cc):
        return {"node": zz * PAIR + yy, "local": xx * PAIR + cc}

    y_peer, c_peer, x_peer = at(z, 1 - y, x, c), at(z, y, x, 1 - c), at(z, y, 1 - x, c)
    d_peer = at(z, y, 1 - x, 1 - c)
    z_peers = [at(partner(z, s, groups), y, x, c) for s in range(1, groups)]
    planes = [partner(z, s, groups) for s in range(groups)]

    def remote(src, dst, send, recv, device):
        return pltpu.make_async_remote_copy(
            src_ref=src, dst_ref=dst, send_sem=send, recv_sem=recv,
            device_id=device, device_id_type=pl.DeviceIdType.MESH,
        )

    loads = [
        pltpu.make_async_copy(tok, xbuf.at[node, :, pl.ds(0, feat)], load_sem.at[0]),
        pltpu.make_async_copy(wg.at[0], vg, load_sem.at[1]),
        pltpu.make_async_copy(wu.at[0], vu, load_sem.at[2]),
        pltpu.make_async_copy(wd.at[0], vd, load_sem.at[3]),
    ]
    for load in loads:
        load.start()
    barrier = pltpu.get_barrier_semaphore()
    peers = [y_peer, c_peer, x_peer, d_peer] + z_peers
    for peer in peers:
        pl.semaphore_signal(barrier, inc=1, device_id=peer, device_id_type=pl.DeviceIdType.MESH)

    place = lax.broadcasted_iota(jnp.int32, (LANES, row_count), 0)
    weight = jnp.zeros((LANES, row_count), F32)
    for k in range(ids.shape[0]):
        expert = ids[k : k + 1, :]
        weight += jnp.where(
            (place == expert) | (place == expert + node_count), mix[k : k + 1, :], 0.0
        )
    head = weight.astype(BF16).astype(F32)
    parts = jnp.where(place < node_count, head, weight - head).astype(BF16)
    same = lax.broadcasted_iota(jnp.int32, (LANES, LANES), 0) == lax.broadcasted_iota(
        jnp.int32, (LANES, LANES), 1
    )
    xbuf[node, :, feat:] = lax.dot_general(
        parts, same.astype(BF16), (((0,), (0,)), ((), ())), preferred_element_type=F32
    ).astype(BF16)
    loads[0].wait()
    pl.semaphore_wait(barrier, len(peers))

    pending = []

    def launch(copy):
        copy.start()
        pending.append(copy)

    launch(remote(xbuf.at[node], xbuf.at[node], a_ysend.at[0], a_recv.at[node], y_peer))
    for s in [s for chunk in chunks for s in chunk if s]:
        launch(
            remote(xbuf.at[node], xbuf.at[node], a_zsend.at[s], a_recv.at[node], z_peers[s - 1])
        )

    def forward(s):
        origin = planes[s] * PAIR + y
        copy = remote(xbuf.at[origin], xbuf.at[origin], a_ysend.at[s], a_recv.at[origin], y_peer)
        copy.wait_recv()
        launch(copy)

    def blocks(s):
        return [planes[step] * PAIR + side for side in range(PAIR) for step in chunks[s]]

    def project(s):
        for step in chunks[s]:
            origin = planes[step] * PAIR + 1 - y
            remote(
                xbuf.at[origin], xbuf.at[origin], a_ysend.at[step], a_recv.at[origin], y_peer
            ).wait_recv()
        if s == 0:
            loads[1].wait()
            loads[2].wait()
        inputs = jnp.concatenate([xbuf[origin, :, :feat] for origin in blocks(s)], axis=0)
        for target, first in ((psend, (1 - c) * half), (pown, c * half)):
            for part in range(PAIR):
                cols = pl.ds(pl.multiple_of(first + part * quarter, quarter), quarter)
                for which, matrix in enumerate((vg, vu)):
                    product = jnp.dot(inputs, matrix[:, cols], preferred_element_type=F32)
                    start = (part * 2 + which) * quarter
                    target[s, :, start : start + quarter] = product.astype(target.dtype)
            if target is psend:
                launch(remote(psend.at[s], precv.at[s], p_send.at[s], p_recv.at[s], c_peer))

    def cross(s):
        remote(psend.at[s], precv.at[s], p_send.at[s], p_recv.at[s], c_peer).wait_recv()
        cols = pl.ds(pl.multiple_of((1 - x) * 2 * quarter, 2 * quarter), 2 * quarter)
        xsend[s] = (pown[s, :, cols] + precv[s, :, cols].astype(F32)).astype(BF16)
        launch(remote(xsend.at[s], xrecv.at[s], x_send.at[s], x_recv.at[s], x_peer))

    def activate(s):
        remote(xsend.at[s], xrecv.at[s], x_send.at[s], x_recv.at[s], x_peer).wait_recv()
        cols = pl.ds(pl.multiple_of(x * 2 * quarter, 2 * quarter), 2 * quarter)
        total = pown[s, :, cols] + precv[s, :, cols].astype(F32) + xrecv[s].astype(F32)
        gate, up = total[:, :quarter], total[:, quarter:]
        act[s, mine] = (gate / (1.0 + jnp.exp(-gate)) * up).astype(BF16)
        for k, peer in enumerate((d_peer, x_peer, c_peer)):
            launch(
                remote(act.at[s, mine], act.at[s, mine], t_send.at[s, k], t_recv.at[s, mine], peer)
            )

    def down(s):
        for k, (cc, xx) in enumerate(((1 - c, 1 - x), (c, 1 - x), (1 - c, x))):
            slot = cc * PAIR + xx
            remote(
                act.at[s, slot], act.at[s, slot], t_send.at[s, k], t_recv.at[s, slot], d_peer
            ).wait_recv()
        if s == 0:
            loads[3].wait()
        hidden = jnp.concatenate([act[s, q] for q in range(PAIR * PAIR)], axis=1)
        scales = jnp.concatenate([xbuf[origin, :, feat:] for origin in blocks(s)], axis=0)
        scales = scales.astype(F32)
        lanes = lax.broadcasted_iota(jnp.int32, scales.shape, 1)
        mine_only = (lanes == node) | (lanes == node + node_count)
        scale = jnp.sum(jnp.where(mine_only, scales, 0.0), axis=1, keepdims=True)
        width = min(feat_out, 2 * LANES)
        for start in range(0, feat_out, width):
            result = jnp.dot(hidden, vd[:, start : start + width], preferred_element_type=F32)
            scaled = result.astype(BF16).astype(F32) * scale
            scaled = scaled.reshape(PAIR, len(chunks[s]), row_count, width)
            for k, step in enumerate(chunks[s]):
                ykeep[step, :, :, start : start + width] = scaled[:, k]
                ysend[step, :, :, start : start + width] = scaled[:, k].astype(BF16)
        for step in chunks[s]:
            launch(returning(step))

    def returning(step):
        return remote(
            ysend.at[step, 1 - y], yrecv.at[step], y_send.at[step], y_recv.at[step], y_peer
        )

    def give_back(s):
        for step in chunks[s]:
            returning(step).wait_recv()
            total = ykeep[step, y] + yrecv[step].astype(F32)
            if step == 0:
                zown[...] = total
            else:
                zsend[step] = total.astype(BF16)
                launch(
                    remote(
                        zsend.at[step], zrecv.at[z], z_send.at[step], z_recv.at[z],
                        z_peers[step - 1],
                    )
                )

    for s in range(len(chunks) + 2):
        if s < len(chunks):
            for step in chunks[s]:
                if step:
                    forward(step)
            project(s)
        if 0 < s <= len(chunks):
            activate(s - 1)
        if s < len(chunks):
            cross(s)
        if 0 < s <= len(chunks):
            down(s - 1)
        if s > 1:
            give_back(s - 2)

    total = zown[...]
    for s in range(1, groups):
        origin = planes[s]
        remote(
            zsend.at[s], zrecv.at[origin], z_send.at[s], z_recv.at[origin], z_peers[s - 1]
        ).wait_recv()
        total = total + zrecv[origin].astype(F32)
    out[...] = total.astype(BF16)
    for copy in pending:
        copy.wait_send()


def fused_body(tokens, node_ids, mix_weights, w_gate, w_up, w_down):
    row_count, feat = tokens.shape
    node_count = lax.axis_size("node")
    hid, feat_out = w_down.shape[1], w_down.shape[2]
    groups = node_count // PAIR
    cuts = chunks_of(groups)
    count, rows = len(cuts), PAIR * row_count * len(cuts[0])
    half = hid // PAIR
    quarters = PAIR * PAIR
    anywhere = pl.BlockSpec(memory_space=pl.ANY)
    vmem = pl.BlockSpec(memory_space=pltpu.VMEM)
    dma = pltpu.SemaphoreType.DMA
    return pl.pallas_call(
        fused_kernel,
        out_shape=jax.ShapeDtypeStruct((row_count, feat_out), BF16),
        in_specs=[anywhere, vmem, vmem, anywhere, anywhere, anywhere],
        out_specs=vmem,
        scratch_shapes=[
            pltpu.VMEM((node_count, row_count, feat + LANES), BF16),
            pltpu.VMEM((feat, hid), BF16),
            pltpu.VMEM((feat, hid), BF16),
            pltpu.VMEM((hid, feat_out), BF16),
            pltpu.VMEM((count, rows, 2 * half), BF16),
            pltpu.VMEM((count, rows, 2 * half), BF16),
            pltpu.VMEM((count, rows, 2 * half), F32),
            pltpu.VMEM((count, rows, half), BF16),
            pltpu.VMEM((count, rows, half), BF16),
            pltpu.VMEM((count, quarters, rows, hid // quarters), BF16),
            pltpu.VMEM((groups, PAIR, row_count, feat_out), BF16),
            pltpu.VMEM((groups, PAIR, row_count, feat_out), F32),
            pltpu.VMEM((groups, row_count, feat_out), BF16),
            pltpu.VMEM((groups, row_count, feat_out), BF16),
            pltpu.VMEM((groups, row_count, feat_out), BF16),
            pltpu.VMEM((row_count, feat_out), F32),
            dma((4,)),
            dma((groups,)),
            dma((groups,)),
            dma((node_count,)),
            dma((groups,)),
            dma((groups,)),
            dma((groups,)),
            dma((groups,)),
            dma((groups, quarters - 1)),
            dma((groups, quarters)),
            dma((groups,)),
            dma((groups,)),
            dma((groups,)),
            dma((groups,)),
        ],
        compiler_params=pltpu.CompilerParams(
            collective_id=0, has_side_effects=True, vmem_limit_bytes=VMEM_BYTES
        ),
        cost_estimate=pl.CostEstimate(
            flops=2 * node_count * row_count * hid * (2 * feat + feat_out),
            bytes_accessed=2 * hid * (2 * feat + feat_out),
            transcendentals=node_count * row_count * hid // quarters,
        ),
    )(tokens, node_ids.T, mix_weights.T, w_gate, w_up, w_down)


def slot_body(slot_cap, tokens, node_ids, mix_weights, w_gate, w_up, w_down):
    row_count, feat_width = tokens.shape
    pick_count = node_ids.shape[1]
    node_count = lax.axis_size("node")
    slot_total = node_count * slot_cap
    flat_ids = node_ids.reshape(-1)
    hit_table = (flat_ids[:, None] == jnp.arange(node_count, dtype=jnp.int32)[None, :]).astype(
        jnp.int32
    )
    earlier = jnp.cumsum(hit_table, axis=0) - hit_table
    slot_rank = jnp.sum(earlier * hit_table, axis=1)
    position = flat_ids * slot_cap + slot_rank
    slot_table = jnp.arange(slot_total, dtype=jnp.int32)[:, None] == position[None, :]
    dispatch = jnp.any(slot_table.reshape(slot_total, row_count, pick_count), axis=2).astype(
        jnp.bfloat16
    )
    outbound = jnp.dot(dispatch, tokens, preferred_element_type=jnp.float32).astype(jnp.bfloat16)
    outbound = outbound.reshape(node_count, slot_cap, feat_width)
    inbound = lax.all_to_all(outbound, "node", split_axis=0, concat_axis=0, tiled=True)
    inbound = inbound.reshape(slot_total, feat_width)
    gate_part = jnp.dot(inbound, w_gate[0], preferred_element_type=jnp.float32)
    up_part = jnp.dot(inbound, w_up[0], preferred_element_type=jnp.float32)
    gate_whole, up_whole = (
        lax.psum(gate_part.astype(jnp.bfloat16), "local").astype(jnp.float32),
        lax.psum(up_part.astype(jnp.bfloat16), "local").astype(jnp.float32),
    )
    active = (jax.nn.silu(gate_whole) * up_whole).astype(jnp.bfloat16)
    result = jnp.dot(active, w_down[0], preferred_element_type=jnp.float32)
    expert_out = result.astype(jnp.bfloat16).reshape(node_count, slot_cap, feat_width)
    returned = lax.all_to_all(expert_out, "node", split_axis=0, concat_axis=0, tiled=True)
    returned = returned.reshape(slot_total, feat_width)
    weighting = slot_table.astype(jnp.float32) * mix_weights.reshape(-1)[None, :]
    combine = jnp.sum(weighting.reshape(slot_total, row_count, pick_count), axis=2)
    mixed = lax.dot_general(
        combine,
        returned.astype(jnp.float32),
        (((0,), (0,)), ((), ())),
        precision=lax.Precision.HIGHEST,
    )
    return mixed.astype(jnp.bfloat16)


def body(tokens, node_ids, mix_weights, w_gate, w_up, w_down):
    row_count, pick_count = node_ids.shape
    node_count, local_count = lax.axis_size("node"), lax.axis_size("local")
    slot_cap = max(2, 2 * row_count * pick_count // node_count)
    args = (tokens, node_ids, mix_weights, w_gate, w_up, w_down)
    paired = node_count % PAIR == 0 and (node_count // PAIR) % 2 == 0
    whole_rows = slot_cap >= row_count and paired and 2 * node_count <= LANES
    if whole_rows and local_count == PAIR * PAIR:
        return fused_body(*args)
    return slot_body(slot_cap, *args)


def solution(mesh):
    return jax.shard_map(
        body,
        mesh=mesh,
        in_specs=(
            P("node", "local"),
            P("node", None),
            P("node", None),
            P("node", "local", None),
            P("node", "local", None),
            P("node", None, "local"),
        ),
        out_specs=P("node", "local"),
        check_vma=False,
    )
```

```python
import functools

import jax
import jax.numpy as jnp
from jax import lax
from jax.experimental import pallas as pl
from jax.experimental.pallas import tpu as pltpu
from jax.sharding import PartitionSpec as P

PAIR = 2
LANES = 128
VMEM_BYTES = 60 * 1024 * 1024
F32 = jnp.float32
BF16 = jnp.bfloat16


def partner(index, step, count):
    if count & (count - 1):
        return lax.rem(index + step, count)
    result, bit = 0, 1
    while bit < count:
        digit = lax.rem(index // bit, 2)
        result = result + (1 - digit if step & bit else digit) * bit
        bit *= 2
    return result


def chunks_of(groups):
    middle = groups // 2
    parts = [0], list(range(middle, 0, -1)), list(range(middle + 1, groups))
    return [part for part in parts if part]


def fused_kernel(
    tok, ids, mix, wg, wu, wd, out,
    xbuf, vg, vu, vd, psend, precv, pown, xsend, xrecv, act, ysend, ykeep, yrecv,
    zsend, zrecv, zown,
    load_sem, a_zsend, a_ysend, a_recv, p_send, p_recv, x_send, x_recv,
    t_send, t_recv, y_send, y_recv, z_send, z_recv,
):
    node_count, row_count, wide = xbuf.shape
    feat = wide - LANES
    groups = node_count // PAIR
    chunks = chunks_of(groups)
    sizes = [PAIR * row_count * len(chunk) for chunk in chunks]
    hid = vg.shape[1]
    half, quarter = hid // PAIR, hid // (PAIR * PAIR)
    feat_out = vd.shape[1]
    node, local = lax.axis_index("node"), lax.axis_index("local")
    z, y = node // PAIR, lax.rem(node, PAIR)
    x, c = local // PAIR, lax.rem(local, PAIR)
    mine = c * PAIR + x

    def at(zz, yy, xx, cc):
        return {"node": zz * PAIR + yy, "local": xx * PAIR + cc}

    y_peer, c_peer, x_peer = at(z, 1 - y, x, c), at(z, y, x, 1 - c), at(z, y, 1 - x, c)
    d_peer = at(z, y, 1 - x, 1 - c)
    z_peers = [at(partner(z, s, groups), y, x, c) for s in range(1, groups)]
    planes = [partner(z, s, groups) for s in range(groups)]

    def remote(src, dst, send, recv, device):
        return pltpu.make_async_remote_copy(
            src_ref=src, dst_ref=dst, send_sem=send, recv_sem=recv,
            device_id=device, device_id_type=pl.DeviceIdType.MESH,
        )

    loads = [
        pltpu.make_async_copy(tok, xbuf.at[node, :, pl.ds(0, feat)], load_sem.at[0]),
        pltpu.make_async_copy(wg.at[0], vg, load_sem.at[1]),
        pltpu.make_async_copy(wu.at[0], vu, load_sem.at[2]),
        pltpu.make_async_copy(wd.at[0], vd, load_sem.at[3]),
    ]
    loads[0].start()
    barrier = pltpu.get_barrier_semaphore()
    peers = [y_peer, c_peer, x_peer, d_peer] + z_peers
    for peer in peers:
        pl.semaphore_signal(barrier, inc=1, device_id=peer, device_id_type=pl.DeviceIdType.MESH)

    place = lax.broadcasted_iota(jnp.int32, (LANES, row_count), 0)
    weight = jnp.zeros((LANES, row_count), F32)
    for k in range(ids.shape[0]):
        expert = ids[k : k + 1, :]
        weight += jnp.where(
            (place == expert) | (place == expert + node_count), mix[k : k + 1, :], 0.0
        )
    head = weight.astype(BF16).astype(F32)
    parts = jnp.where(place < node_count, head, weight - head).astype(BF16)
    same = lax.broadcasted_iota(jnp.int32, (LANES, LANES), 0) == lax.broadcasted_iota(
        jnp.int32, (LANES, LANES), 1
    )
    xbuf[node, :, feat:] = lax.dot_general(
        parts, same.astype(BF16), (((0,), (0,)), ((), ())), preferred_element_type=F32
    ).astype(BF16)
    loads[0].wait()
    loads[1].start()
    loads[2].start()
    pl.semaphore_wait(barrier, len(peers))

    pending = []

    def launch(copy):
        copy.start()
        pending.append(copy)

    launch(remote(xbuf.at[node], xbuf.at[node], a_ysend.at[0], a_recv.at[node], y_peer))
    for s in [s for chunk in chunks for s in chunk if s]:
        launch(
            remote(xbuf.at[node], xbuf.at[node], a_zsend.at[s], a_recv.at[node], z_peers[s - 1])
        )

    loads[3].start()

    def span(ref, s):
        return ref.at[s, pl.ds(0, sizes[s])]

    def to_core(s):
        return remote(span(psend, s), span(precv, s), p_send.at[s], p_recv.at[s], c_peer)

    def to_chip(s):
        return remote(span(xsend, s), span(xrecv, s), x_send.at[s], x_recv.at[s], x_peer)

    def share(s, k, slot, peer):
        block = act.at[s, slot, pl.ds(0, sizes[s])]
        return remote(block, block, t_send.at[s, k], t_recv.at[s, slot], peer)

    def forward(s):
        origin = planes[s] * PAIR + y
        copy = remote(xbuf.at[origin], xbuf.at[origin], a_ysend.at[s], a_recv.at[origin], y_peer)
        copy.wait_recv()
        launch(copy)

    def blocks(s):
        return [planes[step] * PAIR + side for side in range(PAIR) for step in chunks[s]]

    def project(s):
        for step in chunks[s]:
            origin = planes[step] * PAIR + 1 - y
            remote(
                xbuf.at[origin], xbuf.at[origin], a_ysend.at[step], a_recv.at[origin], y_peer
            ).wait_recv()
        if s == 0:
            loads[1].wait()
            loads[2].wait()
        inputs = jnp.concatenate([xbuf[origin, :, :feat] for origin in blocks(s)], axis=0)
        for target, first in ((psend, (1 - c) * half), (pown, c * half)):
            for part in range(PAIR):
                cols = pl.ds(pl.multiple_of(first + part * quarter, quarter), quarter)
                for which, matrix in enumerate((vg, vu)):
                    product = jnp.dot(inputs, matrix[:, cols], preferred_element_type=F32)
                    start = (part * 2 + which) * quarter
                    target[s, : sizes[s], start : start + quarter] = product.astype(target.dtype)
            if target is psend:
                launch(to_core(s))

    def cross(s):
        to_core(s).wait_recv()
        n = sizes[s]
        cols = pl.ds(pl.multiple_of((1 - x) * 2 * quarter, 2 * quarter), 2 * quarter)
        xsend[s, :n] = (pown[s, :n, cols] + precv[s, :n, cols].astype(F32)).astype(BF16)
        launch(to_chip(s))

    def activate(s):
        to_chip(s).wait_recv()
        n = sizes[s]
        cols = pl.ds(pl.multiple_of(x * 2 * quarter, 2 * quarter), 2 * quarter)
        total = pown[s, :n, cols] + precv[s, :n, cols].astype(F32) + xrecv[s, :n].astype(F32)
        gate, up = total[:, :quarter], total[:, quarter:]
        act[s, mine, :n] = (gate / (1.0 + jnp.exp(-gate)) * up).astype(BF16)
        for k, peer in enumerate((d_peer, x_peer, c_peer)):
            launch(share(s, k, mine, peer))

    def down(s):
        for k, (cc, xx) in enumerate(((1 - c, 1 - x), (c, 1 - x), (1 - c, x))):
            share(s, k, cc * PAIR + xx, d_peer).wait_recv()
        if s == 0:
            loads[3].wait()
        hidden = jnp.concatenate([act[s, q, : sizes[s]] for q in range(PAIR * PAIR)], axis=1)
        scales = jnp.concatenate([xbuf[origin, :, feat:] for origin in blocks(s)], axis=0)
        scales = scales.astype(F32)
        lanes = lax.broadcasted_iota(jnp.int32, scales.shape, 1)
        mine_only = (lanes == node) | (lanes == node + node_count)
        scale = jnp.sum(jnp.where(mine_only, scales, 0.0), axis=1, keepdims=True)
        width = min(feat_out, 2 * LANES)
        for start in range(0, feat_out, width):
            result = jnp.dot(hidden, vd[:, start : start + width], preferred_element_type=F32)
            scaled = result.astype(BF16).astype(F32) * scale
            scaled = scaled.reshape(PAIR, len(chunks[s]), row_count, width)
            for k, step in enumerate(chunks[s]):
                ykeep[step, :, :, start : start + width] = scaled[:, k]
                ysend[step, :, :, start : start + width] = scaled[:, k].astype(BF16)
        for step in chunks[s]:
            launch(returning(step))

    def returning(step):
        return remote(
            ysend.at[step, 1 - y], yrecv.at[step], y_send.at[step], y_recv.at[step], y_peer
        )

    def give_back(s):
        for step in chunks[s]:
            returning(step).wait_recv()
            total = ykeep[step, y] + yrecv[step].astype(F32)
            if step == 0:
                zown[...] = total
            else:
                zsend[step] = total.astype(BF16)
                launch(
                    remote(
                        zsend.at[step], zrecv.at[z], z_send.at[step], z_recv.at[z],
                        z_peers[step - 1],
                    )
                )

    project(0)
    cross(0)
    for chunk in chunks[1:]:
        for step in chunk:
            forward(step)
    activate(0)
    for s in range(1, len(chunks)):
        project(s)
        if s > 1:
            activate(s - 1)
        cross(s)
    down(0)
    give_back(0)
    last = len(chunks) - 1
    for s in range(1, last):
        down(s)
    if last > 0:
        activate(last)
        for s in range(1, last):
            give_back(s)
        down(last)
        give_back(last)

    total = zown[...]
    for s in range(1, groups):
        origin = planes[s]
        remote(
            zsend.at[s], zrecv.at[origin], z_send.at[s], z_recv.at[origin], z_peers[s - 1]
        ).wait_recv()
        total = total + zrecv[origin].astype(F32)
    out[...] = total.astype(BF16)
    for copy in pending:
        copy.wait_send()


def fused_body(tokens, node_ids, mix_weights, w_gate, w_up, w_down):
    row_count, feat = tokens.shape
    node_count = lax.axis_size("node")
    hid, feat_out = w_down.shape[1], w_down.shape[2]
    groups = node_count // PAIR
    cuts = chunks_of(groups)
    count, rows = len(cuts), PAIR * row_count * max(len(cut) for cut in cuts)
    half = hid // PAIR
    quarters = PAIR * PAIR
    anywhere = pl.BlockSpec(memory_space=pl.ANY)
    vmem = pl.BlockSpec(memory_space=pltpu.VMEM)
    dma = pltpu.SemaphoreType.DMA
    return pl.pallas_call(
        fused_kernel,
        out_shape=jax.ShapeDtypeStruct((row_count, feat_out), BF16),
        in_specs=[anywhere, vmem, vmem, anywhere, anywhere, anywhere],
        out_specs=vmem,
        scratch_shapes=[
            pltpu.VMEM((node_count, row_count, feat + LANES), BF16),
            pltpu.VMEM((feat, hid), BF16),
            pltpu.VMEM((feat, hid), BF16),
            pltpu.VMEM((hid, feat_out), BF16),
            pltpu.VMEM((count, rows, 2 * half), BF16),
            pltpu.VMEM((count, rows, 2 * half), BF16),
            pltpu.VMEM((count, rows, 2 * half), F32),
            pltpu.VMEM((count, rows, half), BF16),
            pltpu.VMEM((count, rows, half), BF16),
            pltpu.VMEM((count, quarters, rows, hid // quarters), BF16),
            pltpu.VMEM((groups, PAIR, row_count, feat_out), BF16),
            pltpu.VMEM((groups, PAIR, row_count, feat_out), F32),
            pltpu.VMEM((groups, row_count, feat_out), BF16),
            pltpu.VMEM((groups, row_count, feat_out), BF16),
            pltpu.VMEM((groups, row_count, feat_out), BF16),
            pltpu.VMEM((row_count, feat_out), F32),
            dma((4,)),
            dma((groups,)),
            dma((groups,)),
            dma((node_count,)),
            dma((groups,)),
            dma((groups,)),
            dma((groups,)),
            dma((groups,)),
            dma((groups, quarters - 1)),
            dma((groups, quarters)),
            dma((groups,)),
            dma((groups,)),
            dma((groups,)),
            dma((groups,)),
        ],
        compiler_params=pltpu.CompilerParams(
            collective_id=0, has_side_effects=True, vmem_limit_bytes=VMEM_BYTES
        ),
        cost_estimate=pl.CostEstimate(
            flops=2 * node_count * row_count * hid * (2 * feat + feat_out),
            bytes_accessed=2 * hid * (2 * feat + feat_out),
            transcendentals=node_count * row_count * hid // quarters,
        ),
    )(tokens, node_ids.T, mix_weights.T, w_gate, w_up, w_down)


def slot_body(slot_cap, tokens, node_ids, mix_weights, w_gate, w_up, w_down):
    row_count, feat_width = tokens.shape
    pick_count = node_ids.shape[1]
    node_count = lax.axis_size("node")
    slot_total = node_count * slot_cap
    flat_ids = node_ids.reshape(-1)
    hit_table = (flat_ids[:, None] == jnp.arange(node_count, dtype=jnp.int32)[None, :]).astype(
        jnp.int32
    )
    earlier = jnp.cumsum(hit_table, axis=0) - hit_table
    slot_rank = jnp.sum(earlier * hit_table, axis=1)
    position = flat_ids * slot_cap + slot_rank
    slot_table = jnp.arange(slot_total, dtype=jnp.int32)[:, None] == position[None, :]
    dispatch = jnp.any(slot_table.reshape(slot_total, row_count, pick_count), axis=2).astype(
        jnp.bfloat16
    )
    outbound = jnp.dot(dispatch, tokens, preferred_element_type=jnp.float32).astype(jnp.bfloat16)
    outbound = outbound.reshape(node_count, slot_cap, feat_width)
    inbound = lax.all_to_all(outbound, "node", split_axis=0, concat_axis=0, tiled=True)
    inbound = inbound.reshape(slot_total, feat_width)
    gate_part = jnp.dot(inbound, w_gate[0], preferred_element_type=jnp.float32)
    up_part = jnp.dot(inbound, w_up[0], preferred_element_type=jnp.float32)
    gate_whole, up_whole = (
        lax.psum(gate_part.astype(jnp.bfloat16), "local").astype(jnp.float32),
        lax.psum(up_part.astype(jnp.bfloat16), "local").astype(jnp.float32),
    )
    active = (jax.nn.silu(gate_whole) * up_whole).astype(jnp.bfloat16)
    result = jnp.dot(active, w_down[0], preferred_element_type=jnp.float32)
    expert_out = result.astype(jnp.bfloat16).reshape(node_count, slot_cap, feat_width)
    returned = lax.all_to_all(expert_out, "node", split_axis=0, concat_axis=0, tiled=True)
    returned = returned.reshape(slot_total, feat_width)
    weighting = slot_table.astype(jnp.float32) * mix_weights.reshape(-1)[None, :]
    combine = jnp.sum(weighting.reshape(slot_total, row_count, pick_count), axis=2)
    mixed = lax.dot_general(
        combine,
        returned.astype(jnp.float32),
        (((0,), (0,)), ((), ())),
        precision=lax.Precision.HIGHEST,
    )
    return mixed.astype(jnp.bfloat16)


def body(tokens, node_ids, mix_weights, w_gate, w_up, w_down):
    row_count, pick_count = node_ids.shape
    node_count, local_count = lax.axis_size("node"), lax.axis_size("local")
    slot_cap = max(2, 2 * row_count * pick_count // node_count)
    args = (tokens, node_ids, mix_weights, w_gate, w_up, w_down)
    paired = node_count % PAIR == 0 and (node_count // PAIR) % 2 == 0
    whole_rows = slot_cap >= row_count and paired and 2 * node_count <= LANES
    if whole_rows and local_count == PAIR * PAIR:
        return fused_body(*args)
    return slot_body(slot_cap, *args)


def solution(mesh):
    return jax.shard_map(
        body,
        mesh=mesh,
        in_specs=(
            P("node", "local"),
            P("node", None),
            P("node", None),
            P("node", "local", None),
            P("node", "local", None),
            P("node", None, "local"),
        ),
        out_specs=P("node", "local"),
        check_vma=False,
    )
```

```python
import functools

import jax
import jax.numpy as jnp
from jax import lax
from jax.experimental import pallas as pl
from jax.experimental.pallas import tpu as pltpu
from jax.sharding import PartitionSpec as P

PAIR = 2
LANES = 128
VMEM_BYTES = 60 * 1024 * 1024
F32 = jnp.float32
BF16 = jnp.bfloat16


def partner(index, step, count):
    if count & (count - 1):
        return lax.rem(index + step, count)
    result, bit = 0, 1
    while bit < count:
        digit = lax.rem(index // bit, 2)
        result = result + (1 - digit if step & bit else digit) * bit
        bit *= 2
    return result


def chunks_of(groups):
    return [[step] for step in range(groups)]


def fused_kernel(
    tok, ids, mix, wg, wu, wd, out,
    xbuf, vg, vu, vd, psend, precv, pown, xsend, xrecv, act, ysend, ykeep, yrecv,
    zsend, zrecv, zown,
    load_sem, a_zsend, a_ysend, a_recv, p_send, p_recv, x_send, x_recv,
    t_send, t_recv, y_send, y_recv, z_send, z_recv,
):
    node_count, row_count, wide = xbuf.shape
    feat = wide - LANES
    groups = node_count // PAIR
    chunks = chunks_of(groups)
    sizes = [PAIR * row_count * len(chunk) for chunk in chunks]
    hid = vg.shape[1]
    half, quarter = hid // PAIR, hid // (PAIR * PAIR)
    feat_out = vd.shape[1]
    node, local = lax.axis_index("node"), lax.axis_index("local")
    z, y = node // PAIR, lax.rem(node, PAIR)
    x, c = local // PAIR, lax.rem(local, PAIR)
    mine = c * PAIR + x

    def at(zz, yy, xx, cc):
        return {"node": zz * PAIR + yy, "local": xx * PAIR + cc}

    y_peer, c_peer, x_peer = at(z, 1 - y, x, c), at(z, y, x, 1 - c), at(z, y, 1 - x, c)
    d_peer = at(z, y, 1 - x, 1 - c)
    z_peers = [at(partner(z, s, groups), y, x, c) for s in range(1, groups)]
    planes = [partner(z, s, groups) for s in range(groups)]

    def remote(src, dst, send, recv, device):
        return pltpu.make_async_remote_copy(
            src_ref=src, dst_ref=dst, send_sem=send, recv_sem=recv,
            device_id=device, device_id_type=pl.DeviceIdType.MESH,
        )

    loads = [
        pltpu.make_async_copy(tok, xbuf.at[node, :, pl.ds(0, feat)], load_sem.at[0]),
        pltpu.make_async_copy(wg.at[0], vg, load_sem.at[1]),
        pltpu.make_async_copy(wu.at[0], vu, load_sem.at[2]),
        pltpu.make_async_copy(wd.at[0], vd, load_sem.at[3]),
    ]
    loads[0].start()
    barrier = pltpu.get_barrier_semaphore()
    peers = [y_peer, c_peer, x_peer, d_peer] + z_peers
    for peer in peers:
        pl.semaphore_signal(barrier, inc=1, device_id=peer, device_id_type=pl.DeviceIdType.MESH)

    place = lax.broadcasted_iota(jnp.int32, (LANES, row_count), 0)
    weight = jnp.zeros((LANES, row_count), F32)
    for k in range(ids.shape[0]):
        expert = ids[k : k + 1, :]
        weight += jnp.where(
            (place == expert) | (place == expert + node_count), mix[k : k + 1, :], 0.0
        )
    head = weight.astype(BF16).astype(F32)
    parts = jnp.where(place < node_count, head, weight - head).astype(BF16)
    same = lax.broadcasted_iota(jnp.int32, (LANES, LANES), 0) == lax.broadcasted_iota(
        jnp.int32, (LANES, LANES), 1
    )
    xbuf[node, :, feat:] = lax.dot_general(
        parts, same.astype(BF16), (((0,), (0,)), ((), ())), preferred_element_type=F32
    ).astype(BF16)
    loads[0].wait()
    loads[1].start()
    loads[2].start()
    pl.semaphore_wait(barrier, len(peers))

    pending = []

    def launch(copy):
        copy.start()
        pending.append(copy)

    launch(remote(xbuf.at[node], xbuf.at[node], a_ysend.at[0], a_recv.at[node], y_peer))
    for s in [s for chunk in chunks for s in chunk if s]:
        launch(
            remote(xbuf.at[node], xbuf.at[node], a_zsend.at[s], a_recv.at[node], z_peers[s - 1])
        )

    loads[3].start()

    def span(ref, s):
        return ref.at[s, pl.ds(0, sizes[s])]

    def to_core(s):
        return remote(span(psend, s), span(precv, s), p_send.at[s], p_recv.at[s], c_peer)

    def to_chip(s):
        return remote(span(xsend, s), span(xrecv, s), x_send.at[s], x_recv.at[s], x_peer)

    def share(s, k, slot, peer):
        block = act.at[s, slot, pl.ds(0, sizes[s])]
        return remote(block, block, t_send.at[s, k], t_recv.at[s, slot], peer)

    def forward(s):
        origin = planes[s] * PAIR + y
        copy = remote(xbuf.at[origin], xbuf.at[origin], a_ysend.at[s], a_recv.at[origin], y_peer)
        copy.wait_recv()
        launch(copy)

    def blocks(s):
        return [planes[step] * PAIR + side for side in range(PAIR) for step in chunks[s]]

    def project(s):
        for step in chunks[s]:
            origin = planes[step] * PAIR + 1 - y
            remote(
                xbuf.at[origin], xbuf.at[origin], a_ysend.at[step], a_recv.at[origin], y_peer
            ).wait_recv()
        if s == 0:
            loads[1].wait()
            loads[2].wait()
        inputs = jnp.concatenate([xbuf[origin, :, :feat] for origin in blocks(s)], axis=0)
        for target, first in ((psend, (1 - c) * half), (pown, c * half)):
            for part in range(PAIR):
                cols = pl.ds(pl.multiple_of(first + part * quarter, quarter), quarter)
                for which, matrix in enumerate((vg, vu)):
                    product = jnp.dot(inputs, matrix[:, cols], preferred_element_type=F32)
                    start = (part * 2 + which) * quarter
                    target[s, : sizes[s], start : start + quarter] = product.astype(target.dtype)
            if target is psend:
                launch(to_core(s))

    def cross(s):
        to_core(s).wait_recv()
        n = sizes[s]
        cols = pl.ds(pl.multiple_of((1 - x) * 2 * quarter, 2 * quarter), 2 * quarter)
        xsend[s, :n] = (pown[s, :n, cols] + precv[s, :n, cols].astype(F32)).astype(BF16)
        launch(to_chip(s))

    def activate(s):
        to_chip(s).wait_recv()
        n = sizes[s]
        cols = pl.ds(pl.multiple_of(x * 2 * quarter, 2 * quarter), 2 * quarter)
        total = pown[s, :n, cols] + precv[s, :n, cols].astype(F32) + xrecv[s, :n].astype(F32)
        gate, up = total[:, :quarter], total[:, quarter:]
        act[s, mine, :n] = (gate / (1.0 + jnp.exp(-gate)) * up).astype(BF16)
        for k, peer in enumerate((d_peer, x_peer, c_peer)):
            launch(share(s, k, mine, peer))

    def down(s):
        for k, (cc, xx) in enumerate(((1 - c, 1 - x), (c, 1 - x), (1 - c, x))):
            share(s, k, cc * PAIR + xx, d_peer).wait_recv()
        if s == 0:
            loads[3].wait()
        hidden = jnp.concatenate([act[s, q, : sizes[s]] for q in range(PAIR * PAIR)], axis=1)
        scales = jnp.concatenate([xbuf[origin, :, feat:] for origin in blocks(s)], axis=0)
        scales = scales.astype(F32)
        lanes = lax.broadcasted_iota(jnp.int32, scales.shape, 1)
        mine_only = (lanes == node) | (lanes == node + node_count)
        scale = jnp.sum(jnp.where(mine_only, scales, 0.0), axis=1, keepdims=True)
        width = min(feat_out, 2 * LANES)
        for start in range(0, feat_out, width):
            result = jnp.dot(hidden, vd[:, start : start + width], preferred_element_type=F32)
            scaled = result.astype(BF16).astype(F32) * scale
            scaled = scaled.reshape(PAIR, len(chunks[s]), row_count, width)
            for k, step in enumerate(chunks[s]):
                ykeep[step, :, :, start : start + width] = scaled[:, k]
                ysend[step, :, :, start : start + width] = scaled[:, k].astype(BF16)
        for step in chunks[s]:
            launch(returning(step))

    def returning(step):
        return remote(
            ysend.at[step, 1 - y], yrecv.at[step], y_send.at[step], y_recv.at[step], y_peer
        )

    def give_back(s):
        for step in chunks[s]:
            returning(step).wait_recv()
            total = ykeep[step, y] + yrecv[step].astype(F32)
            if step == 0:
                zown[...] = total
            else:
                zsend[step] = total.astype(BF16)
                launch(
                    remote(
                        zsend.at[step], zrecv.at[z], z_send.at[step], z_recv.at[z],
                        z_peers[step - 1],
                    )
                )

    if groups > 1:
        forward(1)
    stages = (project, cross, activate, down, give_back)
    for slot in range(groups + len(stages) - 1):
        for delay, stage in enumerate(stages):
            if 0 <= slot - delay < groups:
                stage(slot - delay)
            if delay == 0 and slot + 2 < groups:
                forward(slot + 2)

    total = zown[...]
    for s in range(1, groups):
        origin = planes[s]
        remote(
            zsend.at[s], zrecv.at[origin], z_send.at[s], z_recv.at[origin], z_peers[s - 1]
        ).wait_recv()
        total = total + zrecv[origin].astype(F32)
    out[...] = total.astype(BF16)
    for copy in pending:
        copy.wait_send()


def fused_body(tokens, node_ids, mix_weights, w_gate, w_up, w_down):
    row_count, feat = tokens.shape
    node_count = lax.axis_size("node")
    hid, feat_out = w_down.shape[1], w_down.shape[2]
    groups = node_count // PAIR
    cuts = chunks_of(groups)
    count, rows = len(cuts), PAIR * row_count * max(len(cut) for cut in cuts)
    half = hid // PAIR
    quarters = PAIR * PAIR
    anywhere = pl.BlockSpec(memory_space=pl.ANY)
    vmem = pl.BlockSpec(memory_space=pltpu.VMEM)
    dma = pltpu.SemaphoreType.DMA
    return pl.pallas_call(
        fused_kernel,
        out_shape=jax.ShapeDtypeStruct((row_count, feat_out), BF16),
        in_specs=[anywhere, vmem, vmem, anywhere, anywhere, anywhere],
        out_specs=vmem,
        scratch_shapes=[
            pltpu.VMEM((node_count, row_count, feat + LANES), BF16),
            pltpu.VMEM((feat, hid), BF16),
            pltpu.VMEM((feat, hid), BF16),
            pltpu.VMEM((hid, feat_out), BF16),
            pltpu.VMEM((count, rows, 2 * half), BF16),
            pltpu.VMEM((count, rows, 2 * half), BF16),
            pltpu.VMEM((count, rows, 2 * half), F32),
            pltpu.VMEM((count, rows, half), BF16),
            pltpu.VMEM((count, rows, half), BF16),
            pltpu.VMEM((count, quarters, rows, hid // quarters), BF16),
            pltpu.VMEM((groups, PAIR, row_count, feat_out), BF16),
            pltpu.VMEM((groups, PAIR, row_count, feat_out), F32),
            pltpu.VMEM((groups, row_count, feat_out), BF16),
            pltpu.VMEM((groups, row_count, feat_out), BF16),
            pltpu.VMEM((groups, row_count, feat_out), BF16),
            pltpu.VMEM((row_count, feat_out), F32),
            dma((4,)),
            dma((groups,)),
            dma((groups,)),
            dma((node_count,)),
            dma((groups,)),
            dma((groups,)),
            dma((groups,)),
            dma((groups,)),
            dma((groups, quarters - 1)),
            dma((groups, quarters)),
            dma((groups,)),
            dma((groups,)),
            dma((groups,)),
            dma((groups,)),
        ],
        compiler_params=pltpu.CompilerParams(
            collective_id=0, has_side_effects=True, vmem_limit_bytes=VMEM_BYTES
        ),
        cost_estimate=pl.CostEstimate(
            flops=2 * node_count * row_count * hid * (2 * feat + feat_out),
            bytes_accessed=2 * hid * (2 * feat + feat_out),
            transcendentals=node_count * row_count * hid // quarters,
        ),
    )(tokens, node_ids.T, mix_weights.T, w_gate, w_up, w_down)


def slot_body(slot_cap, tokens, node_ids, mix_weights, w_gate, w_up, w_down):
    row_count, feat_width = tokens.shape
    pick_count = node_ids.shape[1]
    node_count = lax.axis_size("node")
    slot_total = node_count * slot_cap
    flat_ids = node_ids.reshape(-1)
    hit_table = (flat_ids[:, None] == jnp.arange(node_count, dtype=jnp.int32)[None, :]).astype(
        jnp.int32
    )
    earlier = jnp.cumsum(hit_table, axis=0) - hit_table
    slot_rank = jnp.sum(earlier * hit_table, axis=1)
    position = flat_ids * slot_cap + slot_rank
    slot_table = jnp.arange(slot_total, dtype=jnp.int32)[:, None] == position[None, :]
    dispatch = jnp.any(slot_table.reshape(slot_total, row_count, pick_count), axis=2).astype(
        jnp.bfloat16
    )
    outbound = jnp.dot(dispatch, tokens, preferred_element_type=jnp.float32).astype(jnp.bfloat16)
    outbound = outbound.reshape(node_count, slot_cap, feat_width)
    inbound = lax.all_to_all(outbound, "node", split_axis=0, concat_axis=0, tiled=True)
    inbound = inbound.reshape(slot_total, feat_width)
    gate_part = jnp.dot(inbound, w_gate[0], preferred_element_type=jnp.float32)
    up_part = jnp.dot(inbound, w_up[0], preferred_element_type=jnp.float32)
    gate_whole, up_whole = (
        lax.psum(gate_part.astype(jnp.bfloat16), "local").astype(jnp.float32),
        lax.psum(up_part.astype(jnp.bfloat16), "local").astype(jnp.float32),
    )
    active = (jax.nn.silu(gate_whole) * up_whole).astype(jnp.bfloat16)
    result = jnp.dot(active, w_down[0], preferred_element_type=jnp.float32)
    expert_out = result.astype(jnp.bfloat16).reshape(node_count, slot_cap, feat_width)
    returned = lax.all_to_all(expert_out, "node", split_axis=0, concat_axis=0, tiled=True)
    returned = returned.reshape(slot_total, feat_width)
    weighting = slot_table.astype(jnp.float32) * mix_weights.reshape(-1)[None, :]
    combine = jnp.sum(weighting.reshape(slot_total, row_count, pick_count), axis=2)
    mixed = lax.dot_general(
        combine,
        returned.astype(jnp.float32),
        (((0,), (0,)), ((), ())),
        precision=lax.Precision.HIGHEST,
    )
    return mixed.astype(jnp.bfloat16)


def body(tokens, node_ids, mix_weights, w_gate, w_up, w_down):
    row_count, pick_count = node_ids.shape
    node_count, local_count = lax.axis_size("node"), lax.axis_size("local")
    slot_cap = max(2, 2 * row_count * pick_count // node_count)
    args = (tokens, node_ids, mix_weights, w_gate, w_up, w_down)
    paired = node_count % PAIR == 0 and (node_count // PAIR) % 2 == 0
    whole_rows = slot_cap >= row_count and paired and 2 * node_count <= LANES
    if whole_rows and local_count == PAIR * PAIR:
        return fused_body(*args)
    return slot_body(slot_cap, *args)


def solution(mesh):
    return jax.shard_map(
        body,
        mesh=mesh,
        in_specs=(
            P("node", "local"),
            P("node", None),
            P("node", None),
            P("node", "local", None),
            P("node", "local", None),
            P("node", None, "local"),
        ),
        out_specs=P("node", "local"),
        check_vma=False,
    )
```
